32 devices in a mesh: parts: 2 (over x), fsdp: 8 (over z, y), tp: 2 (over core).
Axes of the slice: x: 2, y: 2, z: 4, core: 2. Of those that a mesh axis runs over, the one named last changes fastest.
Arguments:
- inputs_x: bfloat16 [256, 8192], P(('parts', 'fsdp'), 'tp'), parts along dimension 0, may hold values from -6 to 6
- out_grad: bfloat16 [256, 8192], P(('parts', 'fsdp'), 'tp'), parts along dimension 0, may hold values from -6 to 6
- w_gate: bfloat16 [8192, 14336], P(None, ('fsdp', 'tp')), may hold values from -0.0625 to 0.0625
- w_up: bfloat16 [8192, 14336], P(None, ('fsdp', 'tp')), may hold values from -0.0625 to 0.0625
- w_down: bfloat16 [8192, 14336], P(None, ('fsdp', 'tp')), may hold values from -0.046875 to 0.046875
- proj_input: bfloat16 [2, 4096, 64], P('tp', 'fsdp'), may hold values from -0.0625 to 0.0625
- proj_outgrad: bfloat16 [2, 4096, 64], P('tp', 'fsdp'), may hold values from -0.0625 to 0.0625
- proj_gate: bfloat16 [14336, 64], P(('fsdp', 'tp')), may hold values from -0.046875 to 0.046875
- proj_up: bfloat16 [14336, 64], P(('fsdp', 'tp')), may hold values from -0.046875 to 0.046875
- proj_hidden: bfloat16 [14336, 64], P(('fsdp', 'tp')), may hold values from -0.046875 to 0.046875
- index_queries: bfloat16 [8, 4096, 1536], P('fsdp', 'tp'), may hold values from -0.0546875 to 0.0546875
- block_owner: int32 [8], replicated, may hold values from 0 to 7, each once
- example_ids: int32 [16, 16], P('parts'), parts along dimension 0, may hold values from 0 to 3, never falling along the last dimension, each value on 1 to 8 neighbouring positions
Outputs:
- scores: float32 [64, 4096], P(('parts', 'fsdp'), 'tp'), parts along dimension 0
The draws below stay inside these ranges and needn't reach their ends.
There are 2 independent parts, one for each index of `parts`. The reference program is written for one: setup_inputs(seed, part) draws one part's arguments, and reference() takes and returns one part's arrays. A program takes and returns all parts, laid end to end along the dimension named above; an argument that names none is the same for every part. Nothing has to cross between parts.
Inputs may be any that keep to these rules, and one draw needn't show every extreme that they name: block_owner is a permutation: index block b is held at position block_owner[b] of the first dimension of index_queries. `example_ids`: along each row the example numbers never fall.
All inputs are finite; a program needn't handle non-finite values.
Results may differ from the reference program's by a relative error of at most 0.0041.
Values may be sent and summed in bfloat16 or wider, within the bound.
A program may use at most 128 MiB of HBM per device.

```python
import math
import jax
import jax.numpy as jnp
import numpy as np
from jax import lax

D = 8192
FF_WIN = 14336
RANK = 64
EX_DEV = 4
TOK_DEV = 16
QUERIES = 4096
TOKENS = 128
EXAMPLES = 32
BLOCK = 1536
N_FSDP = 8


def steps_of(own_key, extent, split, smallest, high):
    def one(position, blocks):
        heights = jax.random.uniform(jax.random.fold_in(jax.random.fold_in(own_key, 6), position), (blocks,), jnp.float32, smallest / len(split), high / len(split))
        return jnp.repeat(jnp.exp(heights), extent[position] // blocks).reshape((-1,) + (1,) * (len(extent) - position - 1))

    loudness = one(*split[0])
    for cut in split[1:]:
        loudness = loudness * one(*cut)
    return loudness


def split_up(amount, total, bound, lean):
    loads = [(1 << 20) // math.isqrt(grade ** lean) + 1 for grade in range(2, amount + 1)]
    surplus, counts = total - bound - (amount - 1), [1] * (amount - 1)
    while surplus > 0:
        free = [i for i in range(amount - 1) if counts[i] < bound]
        mass, budget = sum([loads[i] for i in free]), surplus
        for i in free:
            addition = min(bound - counts[i], max(1, budget * loads[i] // mass), surplus)
            counts[i] = counts[i] + addition
            surplus = surplus - addition
    return np.array([bound] + counts)


def uneven(stream_key, number_of, total, reach, lean):
    if number_of == 2:
        one = jax.random.randint(stream_key, (), max(1, total - reach), min(reach, total - 1) + 1)
        return jnp.stack([one, total - one])
    tallies = jnp.asarray(split_up(number_of, total, reach, lean), jnp.int32)
    twos = (number_of - 1) // 2
    source_of, receiver = tallies[1:1 + 2 * twos:2], tallies[2:2 + 2 * twos:2]
    margin = jnp.minimum(source_of - 1, reach - receiver)
    shifted = jax.random.randint(jax.random.fold_in(stream_key, 1), (twos,), 0, 1 << 20) % (margin + 1)
    tallies = tallies.at[1:1 + 2 * twos:2].set(source_of - shifted).at[2:2 + 2 * twos:2].set(receiver + shifted)
    return tallies[jax.random.permutation(jax.random.fold_in(stream_key, 2), number_of)]


def noise(own_key, dims, scale, bound, shards=(), kind=jnp.bfloat16):
    loudness = steps_of(own_key, dims, shards, -0.22, 0.18) if shards else 1.0
    array = jax.random.normal(own_key, dims, jnp.float32) * scale * loudness
    return jnp.minimum(jnp.maximum(array, -bound), bound).astype(kind)


def setup_inputs(seed: int = 0, part: int = 0) -> dict:
    splits = jax.random.split(jax.random.key(seed), 14)
    part_splits = jax.random.split(jax.random.fold_in(splits[13], part), 14)
    inputs_x = noise(part_splits[0], (TOKENS, D), 1.0, 6.0, ((0, 8), (1, 2)))
    out_grad = noise(part_splits[1], (TOKENS, D), 1.0, 6.0, ((0, 8), (1, 2)))
    w_gate = noise(splits[2], (D, FF_WIN), D ** -0.5, 0.0625, ((1, 16),))
    w_up = noise(splits[3], (D, FF_WIN), D ** -0.5, 0.0625, ((1, 16),))
    w_down = noise(splits[4], (D, FF_WIN), FF_WIN ** -0.5, 0.046875, ((1, 16),))
    proj_input = noise(splits[5], (2, D // 2, RANK), D ** -0.5, 0.0625, ((0, 2), (1, 8)))
    proj_outgrad = noise(splits[6], (2, D // 2, RANK), D ** -0.5, 0.0625, ((0, 2), (1, 8)))
    proj_gate = noise(splits[7], (FF_WIN, RANK), FF_WIN ** -0.5, 0.046875, ((0, 16),))
    proj_up = noise(splits[8], (FF_WIN, RANK), FF_WIN ** -0.5, 0.046875, ((0, 16),))
    proj_hidden = noise(splits[9], (FF_WIN, RANK), FF_WIN ** -0.5, 0.046875, ((0, 16),))
    index_queries = noise(splits[10], (N_FSDP, QUERIES, BLOCK), (3 * RANK * RANK) ** -0.5, 0.0546875, ((0, 8), (1, 2)))
    block_owner = jax.random.permutation(splits[11], N_FSDP).astype(jnp.int32)
    example_ids = jax.vmap(lambda own: jnp.searchsorted(jnp.cumsum(uneven(own, EX_DEV, TOK_DEV, TOK_DEV // 2, 0)), jnp.arange(TOK_DEV), side="right"))(jax.random.split(part_splits[12], N_FSDP)).reshape((N_FSDP, TOK_DEV)).astype(jnp.int32)
    return dict(inputs_x=inputs_x, out_grad=out_grad, w_gate=w_gate, w_up=w_up, w_down=w_down, proj_input=proj_input, proj_outgrad=proj_outgrad, proj_gate=proj_gate, proj_up=proj_up, proj_hidden=proj_hidden, index_queries=index_queries, block_owner=block_owner, example_ids=example_ids)


highest_precision = lax.Precision.HIGHEST


def silu_terms(gate_pre):
    sigmoid_gate = jax.nn.sigmoid(gate_pre)
    return gate_pre * sigmoid_gate, sigmoid_gate * (1.0 + gate_pre * (1.0 - sigmoid_gate))


def example_grads(factors, ids, ex_count):
    rank_dim = factors.shape[-1] // 5
    a_in = factors[..., :rank_dim]
    g_out = factors[..., rank_dim:2 * rank_dim]
    g_gate = factors[..., 2 * rank_dim:3 * rank_dim]
    g_up = factors[..., 3 * rank_dim:4 * rank_dim]
    a_hid = factors[..., 4 * rank_dim:]
    one_hot = (ids[:, :, None] == jnp.arange(ex_count, dtype=jnp.int32)[None, None, :]).astype(jnp.float32)

    def outer_sums(left_side, right_side):
        return jnp.einsum("nte,nti,ntj->neij", one_hot, left_side, right_side, precision=highest_precision)

    stacked = jnp.stack([outer_sums(a_in, g_gate), outer_sums(a_in, g_up), outer_sums(a_hid, g_out)], axis=2)
    return stacked.reshape(stacked.shape[0] * ex_count, 3 * rank_dim * rank_dim).astype(jnp.bfloat16)


def reference(inputs_x, out_grad, w_gate, w_up, w_down, proj_input, proj_outgrad, proj_gate, proj_up, proj_hidden, index_queries, block_owner, example_ids):
    gate_pre = jnp.dot(inputs_x, w_gate, preferred_element_type=jnp.float32)
    up_pre = jnp.dot(inputs_x, w_up, preferred_element_type=jnp.float32)
    silu_gate, silu_slope = silu_terms(gate_pre)
    hidden = (silu_gate * up_pre).astype(jnp.bfloat16)
    d_hidden = jnp.dot(out_grad, w_down, preferred_element_type=jnp.float32)
    d_gate = (d_hidden * up_pre * silu_slope).astype(jnp.bfloat16)
    d_up = (d_hidden * silu_gate).astype(jnp.bfloat16)
    a_in = jnp.dot(inputs_x, proj_input.reshape(D, RANK), preferred_element_type=jnp.float32)
    g_out = jnp.dot(out_grad, proj_outgrad.reshape(D, RANK), preferred_element_type=jnp.float32)
    g_gate = jnp.dot(d_gate, proj_gate, preferred_element_type=jnp.float32)
    g_up = jnp.dot(d_up, proj_up, preferred_element_type=jnp.float32)
    a_hid = jnp.dot(hidden, proj_hidden, preferred_element_type=jnp.float32)
    factors = jnp.concatenate([a_in, g_out, g_gate, g_up, a_hid], axis=1)
    grads = example_grads(factors.reshape(N_FSDP, TOK_DEV, 5 * RANK), example_ids, EX_DEV)
    blocks = jnp.transpose(grads.reshape(EXAMPLES, N_FSDP, BLOCK), (1, 0, 2))

    def add_block(total, block_pair):
        block_rows, owner_pos = block_pair
        query_block = lax.dynamic_index_in_dim(index_queries, owner_pos, 0, keepdims=False)
        return total + jnp.dot(block_rows, query_block.T, preferred_element_type=jnp.float32), None

    scores, _ = lax.scan(add_block, jnp.zeros((EXAMPLES, QUERIES), jnp.float32), (blocks, block_owner))
    return scores
```

```python
import functools

import jax
import jax.numpy as jnp
from jax import lax
from jax.experimental import pallas as pl
from jax.experimental.pallas import tpu as pltpu
from jax.sharding import PartitionSpec as P

EX_DEV = 4


highest_precision = lax.Precision.HIGHEST


def silu_terms(gate_pre):
    sigmoid_gate = jax.nn.sigmoid(gate_pre)
    return (gate_pre * sigmoid_gate, sigmoid_gate * (1.0 + gate_pre * (1.0 - sigmoid_gate)))


def example_grads(factors, ids, ex_count):
    rank_dim = factors.shape[-1] // 5
    a_in = factors[..., :rank_dim]
    g_out = factors[..., rank_dim : 2 * rank_dim]
    g_gate = factors[..., 2 * rank_dim : 3 * rank_dim]
    g_up = factors[..., 3 * rank_dim : 4 * rank_dim]
    a_hid = factors[..., 4 * rank_dim :]
    one_hot = (ids[:, :, None] == jnp.arange(ex_count, dtype=jnp.int32)[None, None, :]).astype(
        jnp.float32
    )

    def outer_sums(left_side, right_side):
        return jnp.einsum(
            "nte,nti,ntj->neij", one_hot, left_side, right_side, precision=highest_precision
        )

    stacked = jnp.stack(
        [outer_sums(a_in, g_gate), outer_sums(a_in, g_up), outer_sums(a_hid, g_out)], axis=2
    )
    return stacked.reshape(stacked.shape[0] * ex_count, 3 * rank_dim * rank_dim).astype(
        jnp.bfloat16
    )


def matmul(left_side, right_side):
    return jnp.dot(left_side, right_side, preferred_element_type=jnp.float32)


def layer_terms(gate_pre, up_pre, d_hidden, edge_factors, proj_gate, proj_up, proj_hidden):
    silu_gate, silu_slope = silu_terms(gate_pre)
    hidden = (silu_gate * up_pre).astype(jnp.bfloat16)
    d_gate = (d_hidden * up_pre * silu_slope).astype(jnp.bfloat16)
    d_up = (d_hidden * silu_gate).astype(jnp.bfloat16)
    return jnp.concatenate(
        [
            edge_factors,
            matmul(d_gate, proj_gate),
            matmul(d_up, proj_up),
            matmul(hidden, proj_hidden),
        ],
        axis=1,
    )


def shards(
    inputs_x,
    out_grad,
    w_gate,
    w_up,
    w_down,
    proj_input,
    proj_outgrad,
    proj_gate,
    proj_up,
    proj_hidden,
    index_queries,
    block_owner,
    example_ids,
):
    fsdp_pos = lax.axis_index("fsdp")
    core_pos = lax.axis_index("tp")
    half_width = inputs_x.shape[1]
    slice_width = proj_input.shape[1]
    stacked_rows = jnp.stack([inputs_x, out_grad], axis=1)
    p_in = proj_input[0]
    p_out = proj_outgrad[0]
    full_rows = lax.all_gather(stacked_rows, "tp", axis=2, tiled=True)
    edge_start = core_pos * half_width + fsdp_pos * slice_width
    rows_piece = lax.all_gather(full_rows, "fsdp", axis=0, tiled=True)
    x_rows = rows_piece[:, 0]
    dy_rows = rows_piece[:, 1]
    gate_pre = matmul(x_rows, w_gate)
    up_pre = matmul(x_rows, w_up)
    d_hidden = matmul(dy_rows, w_down)
    x_edge = lax.dynamic_slice_in_dim(x_rows, edge_start, slice_width, 1)
    dy_edge = lax.dynamic_slice_in_dim(dy_rows, edge_start, slice_width, 1)
    edge_factors = jnp.concatenate([matmul(x_edge, p_in), matmul(dy_edge, p_out)], axis=1)
    terms_all = layer_terms(
        gate_pre, up_pre, d_hidden, edge_factors, proj_gate, proj_up, proj_hidden
    )
    count_blocks = block_owner.shape[0]
    positions = jnp.arange(count_blocks, dtype=jnp.int32)
    own_factors = lax.psum_scatter(terms_all, ("fsdp", "tp"), scatter_dimension=0, tiled=True)
    device_factors = lax.all_gather(own_factors, "tp", axis=0, tiled=True)
    row_ids = lax.dynamic_slice_in_dim(example_ids, fsdp_pos, 1, 0)
    local_grads = example_grads(device_factors[None], row_ids, EX_DEV)
    inverse = jnp.sum(
        jnp.where(block_owner[:, None] == positions[None, :], positions[:, None], 0), axis=0
    )
    sending = jnp.take(local_grads.reshape(EX_DEV, count_blocks, -1), inverse, axis=1)
    arrived = lax.all_to_all(sending, "fsdp", split_axis=1, concat_axis=0, tiled=True)
    received = arrived.reshape(arrived.shape[0], arrived.shape[2])
    query_block = index_queries[0]
    return lax.psum_scatter(
        lax.dot_general(
            received, query_block, (((1,), (1,)), ((), ())), preferred_element_type=jnp.float32
        ),
        "fsdp",
        scatter_dimension=0,
        tiled=True,
    )


MESH = pl.DeviceIdType.MESH
NY = 2
SUB = 2
QPIECES = 4


def dot_nt(left_side, right_side, precision=None):
    return lax.dot_general(
        left_side,
        right_side,
        (((1,), (1,)), ((), ())),
        preferred_element_type=jnp.float32,
        precision=precision,
    )


def fused_kernel(
    n_fsdp,
    x_hbm,
    dy_hbm,
    wg_hbm,
    wu_hbm,
    wd_hbm,
    pin_hbm,
    pout_hbm,
    pg_hbm,
    pu_hbm,
    ph_hbm,
    q_hbm,
    owner_ref,
    ids_ref,
    out_ref,
    rows,
    w_vmem,
    q_vmem,
    pin,
    pout,
    pg,
    pu,
    ph,
    acc,
    fsend,
    frecv,
    gref,
    gsend,
    grecv,
    gwide,
    ssend,
    srecv,
    own_sem,
    w_sem,
    small_sem,
    gather_send,
    gather_recv,
    sib_recv,
    f_send_sem,
    f_recv_sem,
    g_send_sem,
    g_recv_sem,
    s_send_sem,
    s_recv_sem,
):
    fs = lax.axis_index("fsdp")
    core = lax.axis_index("tp")
    sib = 1 - core
    nz = n_fsdp // NY
    z = fs // NY
    y = lax.rem(fs, NY)
    tok = x_hbm.shape[0]
    wide = rows.shape[-1]
    chunks = 2 * SUB
    ff = wg_hbm.shape[1]

    own_copies = []
    for c in range(chunks):
        source = x_hbm if c < SUB else dy_hbm
        s = c % SUB
        copy = pltpu.make_async_copy(
            source.at[:, pl.ds(s * wide, wide)],
            rows.at[c, core, pl.ds(fs * tok, tok), :],
            own_sem.at[c],
        )
        copy.start()
        own_copies.append(copy)

    def weight_copy(matrix, hbm, s, h):
        span = pl.ds((h * SUB + s) * wide, wide)
        return pltpu.make_async_copy(
            hbm.at[span, :], w_vmem.at[matrix, span, :], w_sem.at[matrix, s * 2 + h]
        )

    weights = {}
    for s in range(SUB):
        for h in range(2):
            for matrix, hbm in ((0, wg_hbm), (1, wu_hbm)):
                weights[matrix, s, h] = weight_copy(matrix, hbm, s, h)
                weights[matrix, s, h].start()
    small = [
        pltpu.make_async_copy(a, b, small_sem.at[i])
        for i, (a, b) in enumerate(
            (
                (pin_hbm.at[0], pin),
                (pout_hbm.at[0], pout),
                (pg_hbm, pg),
                (pu_hbm, pu),
                (ph_hbm, ph),
                (q_hbm.at[0], q_vmem),
            )
        )
    ]
    for copy in small[:5]:
        copy.start()
    for s in range(SUB):
        for h in range(2):
            weights[2, s, h] = weight_copy(2, wd_hbm, s, h)
            weights[2, s, h].start()
    small[5].start()

    barrier = pltpu.get_barrier_semaphore()
    peers = [(d, t) for d in range(n_fsdp) for t in range(2) if d or t]
    for d, t in peers:
        pl.semaphore_signal(
            barrier,
            inc=1,
            device_id={"fsdp": lax.rem(fs + d, n_fsdp), "tp": lax.rem(core + t, 2)},
            device_id_type=MESH,
        )
    pl.semaphore_wait(barrier, len(peers))

    UP, DOWN, ACROSS, SIB = 0, 1, 2, 3

    def piece_copy(c, origin, way):
        target_fs = {UP: fs + NY, DOWN: fs - NY, ACROSS: z * NY + (1 - y), SIB: fs}[way]
        place = rows.at[c, core, pl.ds(origin * tok, tok), :]
        return pltpu.make_async_remote_copy(
            src_ref=place,
            dst_ref=place,
            send_sem=gather_send.at[c, way, origin],
            recv_sem=(sib_recv if way == SIB else gather_recv).at[c, origin],
            device_id={"fsdp": target_fs, "tp": sib if way == SIB else core},
            device_id_type=MESH,
        )

    def wait_piece(c, origin):
        place = rows.at[c, core, pl.ds(origin * tok, tok), :]
        pltpu.make_async_copy(place, place, gather_recv.at[c, origin]).wait()

    def send_own(c):
        own_copies[c].wait()
        piece_copy(c, fs, ACROSS).start()

        @pl.when(z < nz - 1)
        def _():
            piece_copy(c, fs, UP).start()

        @pl.when(z > 0)
        def _():
            piece_copy(c, fs, DOWN).start()

        piece_copy(c, fs, SIB).start()

    def forward_step(c, d):
        if d < nz:

            @pl.when(z - d >= 0)
            def _():
                origin = fs - d * NY
                wait_piece(c, origin)

                @pl.when(z < nz - 1)
                def _():
                    piece_copy(c, origin, UP).start()

                piece_copy(c, origin, ACROSS).start()
                piece_copy(c, origin, SIB).start()

            @pl.when(z + d < nz)
            def _():
                origin = fs + d * NY
                wait_piece(c, origin)

                @pl.when(z > 0)
                def _():
                    piece_copy(c, origin, DOWN).start()

                piece_copy(c, origin, ACROSS).start()
                piece_copy(c, origin, SIB).start()

        beside = z * NY + (1 - y)
        back = d - 1

        @pl.when(z - back >= 0)
        def _():
            origin = beside - back * NY
            wait_piece(c, origin)
            piece_copy(c, origin, SIB).start()

        if back:

            @pl.when(z + back < nz)
            def _():
                origin = beside + back * NY
                wait_piece(c, origin)
                piece_copy(c, origin, SIB).start()

    def wait_sib(c):
        for origin in range(n_fsdp):
            place = rows.at[c, sib, pl.ds(origin * tok, tok), :]
            pltpu.make_async_copy(place, place, sib_recv.at[c, origin]).wait()

    def drain_sends(c):
        for origin in range(n_fsdp):
            oz, oy = origin // NY, origin % NY
            piece_copy(c, origin, SIB).wait_send()

            @pl.when(y == oy)
            def _():
                piece_copy(c, origin, ACROSS).wait_send()

                @pl.when((z >= oz) & (z < nz - 1))
                def _():
                    piece_copy(c, origin, UP).wait_send()

                @pl.when((z <= oz) & (z > 0))
                def _():
                    piece_copy(c, origin, DOWN).wait_send()

    parts = nz
    tile = 512
    tiles = wide // tile

    def multiply(c, part):
        s = c % SUB
        per = 2 // SUB if SUB > 2 else 1
        h, rest = divmod(part, parts // 2)
        share = tiles // (parts // 2)
        matrices = (0, 1) if c < SUB else (2,)
        if rest == 0:
            for matrix in matrices:
                weights[matrix, s, h].wait()

        def body(k, carry):
            start = pl.multiple_of((rest * share + k) * tile, tile)
            left = rows[c, h, :, pl.ds(start, tile)]
            for matrix in matrices:
                base = pl.multiple_of((h * SUB + s) * wide + start, tile)
                acc[matrix] += matmul(left, w_vmem[matrix, pl.ds(base, tile), :])
            return carry

        lax.fori_loop(0, share, body, 0)

    def edge(first_chunk):
        width = pin.shape[0]
        per = wide // width
        at = pl.multiple_of(lax.rem(fs, per) * width, width)
        return rows[first_chunk + fs // per, core, :, pl.ds(at, width)]

    cols = 128

    def middle():
        for copy in small[:5]:
            copy.wait()
        a_hid = jnp.zeros((n_fsdp * tok, ph.shape[1]), jnp.float32)
        for n in range(ff // cols):
            at = slice(n * cols, (n + 1) * cols)
            gate = acc[0, :, at]
            up = acc[1, :, at]
            silu_gate, slope = silu_terms(gate)
            a_hid += matmul((silu_gate * up).astype(jnp.bfloat16), ph[at, :])
            acc[0, :, at] = up * slope
            acc[1, :, at] = silu_gate
        a_in = matmul(edge(0), pin[...])
        fsend[:, 0:128] = jnp.concatenate([a_in, a_hid], axis=1).astype(jnp.bfloat16)

    acc[...] = jnp.zeros_like(acc)
    send_own(0)
    send_own(1)
    for c in range(chunks):
        if c >= 1 and c + 1 < chunks:
            send_own(c + 1)
        for d in range(1, nz + 1):
            forward_step(c, d)
            if c:
                multiply(c - 1, d - 1)
            if c == SUB + 1 and d == 1:
                middle()
        wait_sib(c)
    for part in range(parts):
        multiply(chunks - 1, part)
    g_out = matmul(edge(SUB), pout[...])
    g_gate = jnp.zeros_like(g_out)
    g_up = jnp.zeros_like(g_out)
    for n in range(ff // cols):
        at = slice(n * cols, (n + 1) * cols)
        d_hidden = acc[2, :, at]
        g_gate += matmul((d_hidden * acc[0, :, at]).astype(jnp.bfloat16), pg[at, :])
        g_up += matmul((d_hidden * acc[1, :, at]).astype(jnp.bfloat16), pu[at, :])
    fsend[:, 128:256] = jnp.concatenate([g_gate, g_up], axis=1).astype(jnp.bfloat16)
    fsend[:, 256:384] = jnp.concatenate([g_out, jnp.zeros_like(g_out)], axis=1).astype(
        jnp.bfloat16
    )

    me = fs * 2 + core
    f_copies = []
    for i, (d, t) in enumerate(peers):
        target, target_core = lax.rem(fs + d, n_fsdp), lax.rem(core + t, 2)
        copy = pltpu.make_async_remote_copy(
            src_ref=fsend.at[pl.ds(target * tok, tok), :],
            dst_ref=frecv.at[me],
            send_sem=f_send_sem.at[i],
            recv_sem=f_recv_sem.at[me],
            device_id={"fsdp": target, "tp": target_core},
            device_id_type=MESH,
        )
        copy.start()
        f_copies.append(copy)
    frecv[me] = fsend[pl.ds(fs * tok, tok), :]
    for c in range(chunks):
        drain_sends(c)
    for d, t in peers:
        source = lax.rem(fs + d, n_fsdp) * 2 + lax.rem(core + t, 2)
        place = frecv.at[source]
        pltpu.make_async_copy(place, place, f_recv_sem.at[source]).wait()
    total = jnp.sum(frecv[...].astype(jnp.float32), axis=0)

    rank = pin.shape[1]
    pairs = rank // 2
    a_in, a_hid = total[:, 0:64], total[:, 64:128]
    rights = (total[:, 128:192], total[:, 192:256], total[:, 256:320])
    row = lax.broadcasted_iota(jnp.int32, (pairs * EX_DEV, rank), 0)
    col = lax.broadcasted_iota(jnp.int32, (pairs * EX_DEV, rank), 1)
    token_row = lax.broadcasted_iota(jnp.int32, (pairs * EX_DEV, tok), 0)
    ids = ids_ref[pl.ds(fs, 1), :]
    mask = (lax.rem(token_row, EX_DEV) == ids).astype(jnp.float32)
    picks = [(col == 2 * (row // EX_DEV) + par).astype(jnp.float32) for par in range(2)]
    left_in = [dot_nt(pick, a_in, highest_precision) * mask for pick in picks]
    left_hid = [dot_nt(pick, a_hid, highest_precision) * mask for pick in picks]
    blank = jnp.zeros((tok, rank), jnp.float32)
    for m in range(3):
        lefts = left_hid if m == 2 else left_in
        g = jnp.dot(
            lefts[0],
            jnp.concatenate([rights[m], blank], axis=1),
            preferred_element_type=jnp.float32,
            precision=highest_precision,
        ) + jnp.dot(
            lefts[1],
            jnp.concatenate([blank, rights[m]], axis=1),
            preferred_element_type=jnp.float32,
            precision=highest_precision,
        )
        gref[pl.ds(m * pairs * EX_DEV, pairs * EX_DEV), :] = g

    block_rows = gsend.shape[1]
    for target in range(n_fsdp):
        chosen = jnp.zeros((block_rows, 128), jnp.float32)
        for b in range(n_fsdp):
            keep = (owner_ref[b] == target).astype(jnp.float32)
            chosen += keep * gref[pl.ds(b * block_rows, block_rows), :]
        gsend[target] = chosen.astype(jnp.bfloat16)
    g_copies = []
    for d in range(1, n_fsdp):
        target = lax.rem(fs + d, n_fsdp)
        copy = pltpu.make_async_remote_copy(
            src_ref=gsend.at[target],
            dst_ref=grecv.at[fs],
            send_sem=g_send_sem.at[d],
            recv_sem=g_recv_sem.at[fs],
            device_id={"fsdp": target, "tp": core},
            device_id_type=MESH,
        )
        copy.start()
        g_copies.append(copy)
    grecv[fs] = gsend[fs]
    small[5].wait()
    for copy in f_copies:
        copy.wait_send()
    for d in range(1, n_fsdp):
        source = lax.rem(fs + d, n_fsdp)
        place = grecv.at[source]
        pltpu.make_async_copy(place, place, g_recv_sem.at[source]).wait()
    gwide[...] = grecv[...].astype(jnp.float32)
    left = jnp.concatenate(
        [
            jnp.concatenate(
                [gwide[f, p * EX_DEV : (p + 1) * EX_DEV, :] for f in range(n_fsdp)], axis=0
            )
            for p in range(block_rows // EX_DEV)
        ],
        axis=1,
    ).astype(jnp.bfloat16)
    piece = q_vmem.shape[0] // QPIECES
    scores = [
        dot_nt(left, q_vmem[n * piece : (n + 1) * piece, :]) for n in range(QPIECES)
    ]
    for f in range(n_fsdp):
        ssend[f] = jnp.concatenate(
            [score[f * EX_DEV : (f + 1) * EX_DEV, :] for score in scores], axis=0
        ).astype(jnp.bfloat16)

    s_copies = []
    for d in range(1, n_fsdp):
        target = lax.rem(fs + d, n_fsdp)
        copy = pltpu.make_async_remote_copy(
            src_ref=ssend.at[target],
            dst_ref=srecv.at[fs],
            send_sem=s_send_sem.at[d],
            recv_sem=s_recv_sem.at[fs],
            device_id={"fsdp": target, "tp": core},
            device_id_type=MESH,
        )
        copy.start()
        s_copies.append(copy)
    srecv[fs] = ssend[fs]
    for copy in g_copies:
        copy.wait_send()
    for d in range(1, n_fsdp):
        source = lax.rem(fs + d, n_fsdp)
        place = srecv.at[source]
        pltpu.make_async_copy(place, place, s_recv_sem.at[source]).wait()
    summed = jnp.sum(srecv[...].astype(jnp.float32), axis=0)
    for n in range(QPIECES):
        out_ref[:, n * piece : (n + 1) * piece] = summed[n * EX_DEV : (n + 1) * EX_DEV, :]
    for copy in s_copies:
        copy.wait_send()


def fused_shards(n_fsdp, *args):
    x, _, wg = args[:3]
    pin, pg = args[5], args[7]
    q = args[10]
    tok, half = x.shape
    tokens = n_fsdp * tok
    wide = half // SUB
    depth, ff = wg.shape
    rank = pg.shape[1]
    queries, block = q.shape[1:]
    chunks = 2 * SUB
    block_rows = block // 128 * EX_DEV
    dma = pltpu.SemaphoreType.DMA
    bf16, f32 = jnp.bfloat16, jnp.float32
    hbm = pl.BlockSpec(memory_space=pl.ANY)
    return pl.pallas_call(
        functools.partial(fused_kernel, n_fsdp),
        out_shape=jax.ShapeDtypeStruct((EX_DEV, queries), f32),
        in_specs=[hbm] * 11
        + [pl.BlockSpec(memory_space=pltpu.SMEM), pl.BlockSpec(memory_space=pltpu.VMEM)],
        out_specs=pl.BlockSpec(memory_space=pltpu.VMEM),
        scratch_shapes=[
            pltpu.VMEM((chunks, 2, tokens, wide), bf16),
            pltpu.VMEM((3, depth, ff), bf16),
            pltpu.VMEM((queries, block), bf16),
            pltpu.VMEM(pin.shape[1:], bf16),
            pltpu.VMEM(pin.shape[1:], bf16),
            pltpu.VMEM((ff, rank), bf16),
            pltpu.VMEM((ff, rank), bf16),
            pltpu.VMEM((ff, rank), bf16),
            pltpu.VMEM((3, tokens, ff), f32),
            pltpu.VMEM((tokens, 6 * rank), bf16),
            pltpu.VMEM((2 * n_fsdp, tok, 6 * rank), bf16),
            pltpu.VMEM((n_fsdp * block_rows, 128), f32),
            pltpu.VMEM((n_fsdp, block_rows, 128), bf16),
            pltpu.VMEM((n_fsdp, block_rows, 128), bf16),
            pltpu.VMEM((n_fsdp, block_rows, 128), f32),
            pltpu.VMEM((n_fsdp, QPIECES * EX_DEV, queries // QPIECES), bf16),
            pltpu.VMEM((n_fsdp, QPIECES * EX_DEV, queries // QPIECES), bf16),
            dma((chunks,)),
            dma((3, 2 * SUB)),
            dma((6,)),
            dma((chunks, 4, n_fsdp)),
            dma((chunks, n_fsdp)),
            dma((chunks, n_fsdp)),
            dma((2 * n_fsdp,)),
            dma((2 * n_fsdp,)),
            dma((n_fsdp,)),
            dma((n_fsdp,)),
            dma((n_fsdp,)),
            dma((n_fsdp,)),
        ],
        compiler_params=pltpu.CompilerParams(
            collective_id=0, has_side_effects=True, vmem_limit_bytes=62 * 1024 * 1024
        ),
    )(*args)


def pick_shards(n_fsdp, n_tp):
    def run(*args):
        x, wg, q = args[0], args[2], args[10]
        fits = (
            n_tp == 2
            and n_fsdp == 8
            and x.shape[0] == 16
            and args[7].shape[1] == 64
            and wg.shape[1] % 128 == 0
            and wg.size * 6 + q.size * 2 < 52 * 1024 * 1024
        )
        return fused_shards(n_fsdp, *args) if fits else shards(*args)

    return run


def solution(mesh):
    return jax.shard_map(
        pick_shards(mesh.shape["fsdp"], mesh.shape["tp"]),
        mesh=mesh,
        in_specs=(
            P(("parts", "fsdp"), "tp"),
            P(("parts", "fsdp"), "tp"),
            P(None, ("fsdp", "tp")),
            P(None, ("fsdp", "tp")),
            P(None, ("fsdp", "tp")),
            P("tp", "fsdp", None),
            P("tp", "fsdp", None),
            P(("fsdp", "tp"), None),
            P(("fsdp", "tp"), None),
            P(("fsdp", "tp"), None),
            P("fsdp", "tp", None),
            P(),
            P("parts", None),
        ),
        out_specs=P(("parts", "fsdp"), "tp"),
        check_vma=False,
    )
```

```python
import functools

import jax
import jax.numpy as jnp
from jax import lax
from jax.experimental import pallas as pl
from jax.experimental.pallas import tpu as pltpu
from jax.sharding import PartitionSpec as P

EX_DEV = 4


highest_precision = lax.Precision.HIGHEST


def silu_terms(gate_pre):
    sigmoid_gate = jax.nn.sigmoid(gate_pre)
    return (gate_pre * sigmoid_gate, sigmoid_gate * (1.0 + gate_pre * (1.0 - sigmoid_gate)))


def example_grads(factors, ids, ex_count):
    rank_dim = factors.shape[-1] // 5
    a_in = factors[..., :rank_dim]
    g_out = factors[..., rank_dim : 2 * rank_dim]
    g_gate = factors[..., 2 * rank_dim : 3 * rank_dim]
    g_up = factors[..., 3 * rank_dim : 4 * rank_dim]
    a_hid = factors[..., 4 * rank_dim :]
    one_hot = (ids[:, :, None] == jnp.arange(ex_count, dtype=jnp.int32)[None, None, :]).astype(
        jnp.float32
    )

    def outer_sums(left_side, right_side):
        return jnp.einsum(
            "nte,nti,ntj->neij", one_hot, left_side, right_side, precision=highest_precision
        )

    stacked = jnp.stack(
        [outer_sums(a_in, g_gate), outer_sums(a_in, g_up), outer_sums(a_hid, g_out)], axis=2
    )
    return stacked.reshape(stacked.shape[0] * ex_count, 3 * rank_dim * rank_dim).astype(
        jnp.bfloat16
    )


def matmul(left_side, right_side):
    return jnp.dot(left_side, right_side, preferred_element_type=jnp.float32)


def layer_terms(gate_pre, up_pre, d_hidden, edge_factors, proj_gate, proj_up, proj_hidden):
    silu_gate, silu_slope = silu_terms(gate_pre)
    hidden = (silu_gate * up_pre).astype(jnp.bfloat16)
    d_gate = (d_hidden * up_pre * silu_slope).astype(jnp.bfloat16)
    d_up = (d_hidden * silu_gate).astype(jnp.bfloat16)
    return jnp.concatenate(
        [
            edge_factors,
            matmul(d_gate, proj_gate),
            matmul(d_up, proj_up),
            matmul(hidden, proj_hidden),
        ],
        axis=1,
    )


def shards(
    inputs_x,
    out_grad,
    w_gate,
    w_up,
    w_down,
    proj_input,
    proj_outgrad,
    proj_gate,
    proj_up,
    proj_hidden,
    index_queries,
    block_owner,
    example_ids,
):
    fsdp_pos = lax.axis_index("fsdp")
    core_pos = lax.axis_index("tp")
    half_width = inputs_x.shape[1]
    slice_width = proj_input.shape[1]
    stacked_rows = jnp.stack([inputs_x, out_grad], axis=1)
    p_in = proj_input[0]
    p_out = proj_outgrad[0]
    full_rows = lax.all_gather(stacked_rows, "tp", axis=2, tiled=True)
    edge_start = core_pos * half_width + fsdp_pos * slice_width
    rows_piece = lax.all_gather(full_rows, "fsdp", axis=0, tiled=True)
    x_rows = rows_piece[:, 0]
    dy_rows = rows_piece[:, 1]
    gate_pre = matmul(x_rows, w_gate)
    up_pre = matmul(x_rows, w_up)
    d_hidden = matmul(dy_rows, w_down)
    x_edge = lax.dynamic_slice_in_dim(x_rows, edge_start, slice_width, 1)
    dy_edge = lax.dynamic_slice_in_dim(dy_rows, edge_start, slice_width, 1)
    edge_factors = jnp.concatenate([matmul(x_edge, p_in), matmul(dy_edge, p_out)], axis=1)
    terms_all = layer_terms(
        gate_pre, up_pre, d_hidden, edge_factors, proj_gate, proj_up, proj_hidden
    )
    count_blocks = block_owner.shape[0]
    positions = jnp.arange(count_blocks, dtype=jnp.int32)
    own_factors = lax.psum_scatter(terms_all, ("fsdp", "tp"), scatter_dimension=0, tiled=True)
    device_factors = lax.all_gather(own_factors, "tp", axis=0, tiled=True)
    row_ids = lax.dynamic_slice_in_dim(example_ids, fsdp_pos, 1, 0)
    local_grads = example_grads(device_factors[None], row_ids, EX_DEV)
    inverse = jnp.sum(
        jnp.where(block_owner[:, None] == positions[None, :], positions[:, None], 0), axis=0
    )
    sending = jnp.take(local_grads.reshape(EX_DEV, count_blocks, -1), inverse, axis=1)
    arrived = lax.all_to_all(sending, "fsdp", split_axis=1, concat_axis=0, tiled=True)
    received = arrived.reshape(arrived.shape[0], arrived.shape[2])
    query_block = index_queries[0]
    return lax.psum_scatter(
        lax.dot_general(
            received, query_block, (((1,), (1,)), ((), ())), preferred_element_type=jnp.float32
        ),
        "fsdp",
        scatter_dimension=0,
        tiled=True,
    )


MESH = pl.DeviceIdType.MESH
NY = 2
SUB = 2
QPIECES = 4


def dot_nt(left_side, right_side, precision=None):
    return lax.dot_general(
        left_side,
        right_side,
        (((1,), (1,)), ((), ())),
        preferred_element_type=jnp.float32,
        precision=precision,
    )


def fused_kernel(
    n_fsdp,
    x_hbm,
    dy_hbm,
    wg_hbm,
    wu_hbm,
    wd_hbm,
    pin_hbm,
    pout_hbm,
    pg_hbm,
    pu_hbm,
    ph_hbm,
    q_hbm,
    owner_ref,
    ids_ref,
    out_ref,
    rows,
    w_vmem,
    q_vmem,
    pin,
    pout,
    pg,
    pu,
    ph,
    acc,
    early_send,
    early_recv,
    late_send,
    late_recv,
    pair_send,
    pair_recv,
    gref,
    gsend,
    grecv,
    gwide,
    ssend,
    srecv,
    own_sem,
    w_sem,
    small_sem,
    gather_send,
    gather_recv,
    sib_recv,
    f_send_sem,
    f_recv_sem,
    pair_sem,
    g_send_sem,
    g_recv_sem,
    s_send_sem,
    s_recv_sem,
):
    fs = lax.axis_index("fsdp")
    core = lax.axis_index("tp")
    sib = 1 - core
    nz = n_fsdp // NY
    z = fs // NY
    y = lax.rem(fs, NY)
    tok = x_hbm.shape[0]
    wide = rows.shape[-1]
    chunks = 2 * SUB
    ff = wg_hbm.shape[1]

    own_copies = []
    for c in range(chunks):
        source = x_hbm if c < SUB else dy_hbm
        s = c % SUB
        copy = pltpu.make_async_copy(
            source.at[:, pl.ds(s * wide, wide)],
            rows.at[c, core, pl.ds(fs * tok, tok), :],
            own_sem.at[c],
        )
        copy.start()
        own_copies.append(copy)

    def weight_copy(matrix, hbm, s, h):
        span = pl.ds((h * SUB + s) * wide, wide)
        return pltpu.make_async_copy(
            hbm.at[span, :], w_vmem.at[matrix, span, :], w_sem.at[matrix, s * 2 + h]
        )

    weights = {}
    for s in range(SUB):
        for h in range(2):
            for matrix, hbm in ((0, wg_hbm), (1, wu_hbm)):
                weights[matrix, s, h] = weight_copy(matrix, hbm, s, h)
                weights[matrix, s, h].start()
    small = [
        pltpu.make_async_copy(a, b, small_sem.at[i])
        for i, (a, b) in enumerate(
            (
                (pin_hbm, pin),
                (pout_hbm, pout),
                (pg_hbm, pg),
                (pu_hbm, pu),
                (ph_hbm, ph),
                (q_hbm.at[0], q_vmem),
            )
        )
    ]
    for copy in small[:5]:
        copy.start()
    for s in range(SUB):
        for h in range(2):
            weights[2, s, h] = weight_copy(2, wd_hbm, s, h)
            weights[2, s, h].start()
    small[5].start()

    barrier = pltpu.get_barrier_semaphore()
    peers = [(d, t) for d in range(n_fsdp) for t in range(2) if d or t]
    for d, t in peers:
        pl.semaphore_signal(
            barrier,
            inc=1,
            device_id={"fsdp": lax.rem(fs + d, n_fsdp), "tp": lax.rem(core + t, 2)},
            device_id_type=MESH,
        )
    pl.semaphore_wait(barrier, len(peers))

    UP, DOWN, ACROSS, SIB = 0, 1, 2, 3

    def piece_copy(c, origin, way):
        target_fs = {UP: fs + NY, DOWN: fs - NY, ACROSS: z * NY + (1 - y), SIB: fs}[way]
        place = rows.at[c, core, pl.ds(origin * tok, tok), :]
        return pltpu.make_async_remote_copy(
            src_ref=place,
            dst_ref=place,
            send_sem=gather_send.at[c, way, origin],
            recv_sem=(sib_recv if way == SIB else gather_recv).at[c, origin],
            device_id={"fsdp": target_fs, "tp": sib if way == SIB else core},
            device_id_type=MESH,
        )

    def wait_piece(c, origin):
        place = rows.at[c, core, pl.ds(origin * tok, tok), :]
        pltpu.make_async_copy(place, place, gather_recv.at[c, origin]).wait()

    def send_own(c):
        own_copies[c].wait()
        piece_copy(c, fs, ACROSS).start()

        @pl.when(z < nz - 1)
        def _():
            piece_copy(c, fs, UP).start()

        @pl.when(z > 0)
        def _():
            piece_copy(c, fs, DOWN).start()

        piece_copy(c, fs, SIB).start()

    def forward_step(c, d):
        if d < nz:

            @pl.when(z - d >= 0)
            def _():
                origin = fs - d * NY
                wait_piece(c, origin)

                @pl.when(z < nz - 1)
                def _():
                    piece_copy(c, origin, UP).start()

                piece_copy(c, origin, ACROSS).start()
                piece_copy(c, origin, SIB).start()

            @pl.when(z + d < nz)
            def _():
                origin = fs + d * NY
                wait_piece(c, origin)

                @pl.when(z > 0)
                def _():
                    piece_copy(c, origin, DOWN).start()

                piece_copy(c, origin, ACROSS).start()
                piece_copy(c, origin, SIB).start()

        beside = z * NY + (1 - y)
        back = d - 1

        @pl.when(z - back >= 0)
        def _():
            origin = beside - back * NY
            wait_piece(c, origin)
            piece_copy(c, origin, SIB).start()

        if back:

            @pl.when(z + back < nz)
            def _():
                origin = beside + back * NY
                wait_piece(c, origin)
                piece_copy(c, origin, SIB).start()

    def wait_sib(c):
        for origin in range(n_fsdp):
            place = rows.at[c, sib, pl.ds(origin * tok, tok), :]
            pltpu.make_async_copy(place, place, sib_recv.at[c, origin]).wait()

    def drain_sends(c):
        for origin in range(n_fsdp):
            oz, oy = origin // NY, origin % NY
            piece_copy(c, origin, SIB).wait_send()

            @pl.when(y == oy)
            def _():
                piece_copy(c, origin, ACROSS).wait_send()

                @pl.when((z >= oz) & (z < nz - 1))
                def _():
                    piece_copy(c, origin, UP).wait_send()

                @pl.when((z <= oz) & (z > 0))
                def _():
                    piece_copy(c, origin, DOWN).wait_send()

    parts = nz
    tile = 512
    tiles = wide // tile

    def multiply(c, part):
        s = c % SUB
        per = 2 // SUB if SUB > 2 else 1
        h, rest = divmod(part, parts // 2)
        share = tiles // (parts // 2)
        matrices = (0, 1) if c < SUB else (2,)
        if rest == 0:
            for matrix in matrices:
                weights[matrix, s, h].wait()

        def body(k, carry):
            start = pl.multiple_of((rest * share + k) * tile, tile)
            left = rows[c, h, :, pl.ds(start, tile)]
            for matrix in matrices:
                base = pl.multiple_of((h * SUB + s) * wide + start, tile)
                acc[matrix] += matmul(left, w_vmem[matrix, pl.ds(base, tile), :])
            return carry

        lax.fori_loop(0, share, body, 0)

    def edge(first_chunk):
        width = pin.shape[1]
        per = wide // width
        at = pl.multiple_of(lax.rem(fs, per) * width, width)
        return rows[first_chunk + fs // per, core, :, pl.ds(at, width)]

    f_copies = []

    def send_factors(src, dst, stage):
        for d in range(1, n_fsdp):
            target = lax.rem(fs + d, n_fsdp)
            copy = pltpu.make_async_remote_copy(
                src_ref=src.at[pl.ds(target * tok, tok), :],
                dst_ref=dst.at[fs],
                send_sem=f_send_sem.at[stage, d],
                recv_sem=f_recv_sem.at[stage, fs],
                device_id={"fsdp": target, "tp": core},
                device_id_type=MESH,
            )
            copy.start()
            f_copies.append(copy)
        dst[fs] = src[pl.ds(fs * tok, tok), :]

    def arrive_factors(dst, stage):
        for d in range(1, n_fsdp):
            source = lax.rem(fs + d, n_fsdp)
            place = dst.at[source]
            pltpu.make_async_copy(place, place, f_recv_sem.at[stage, source]).wait()

    cols = 128

    def middle():
        for copy in small[:5]:
            copy.wait()
        a_hid = jnp.zeros((n_fsdp * tok, ph.shape[0]), jnp.float32)
        for n in range(ff // cols):
            at = slice(n * cols, (n + 1) * cols)
            gate = acc[0, :, at]
            up = acc[1, :, at]
            silu_gate, slope = silu_terms(gate)
            a_hid += dot_nt((silu_gate * up).astype(jnp.bfloat16), ph[:, at])
            acc[0, :, at] = up * slope
            acc[1, :, at] = silu_gate
        a_in = dot_nt(edge(0), pin[...])
        early_send[...] = jnp.concatenate([a_in, a_hid], axis=1)
        send_factors(early_send, early_recv, 0)

    acc[...] = jnp.zeros_like(acc)
    send_own(0)
    send_own(1)
    for c in range(chunks):
        if c >= 1 and c + 1 < chunks:
            send_own(c + 1)
        for d in range(1, nz + 1):
            forward_step(c, d)
            if c:
                multiply(c - 1, d - 1)
            if c == SUB + 1 and d == 1:
                middle()
        wait_sib(c)
    for part in range(parts):
        multiply(chunks - 1, part)
    g_out = dot_nt(edge(SUB), pout[...])
    g_gate = jnp.zeros_like(g_out)
    g_up = jnp.zeros_like(g_out)
    for n in range(ff // cols):
        at = slice(n * cols, (n + 1) * cols)
        d_hidden = acc[2, :, at]
        g_gate += dot_nt((d_hidden * acc[0, :, at]).astype(jnp.bfloat16), pg[:, at])
        g_up += dot_nt((d_hidden * acc[1, :, at]).astype(jnp.bfloat16), pu[:, at])
    late_send[:, 0:128] = jnp.concatenate([g_gate, g_up], axis=1)
    late_send[:, 128:256] = jnp.concatenate([g_out, jnp.zeros_like(g_out)], axis=1)

    send_factors(late_send, late_recv, 1)
    for c in range(chunks):
        drain_sends(c)
    arrive_factors(early_recv, 0)
    pair_send[:, 0:128] = jnp.sum(early_recv[...], axis=0)
    arrive_factors(late_recv, 1)
    pair_send[:, 128:384] = jnp.sum(late_recv[...], axis=0)
    pair_copy = pltpu.make_async_remote_copy(
        src_ref=pair_send,
        dst_ref=pair_recv,
        send_sem=pair_sem.at[0],
        recv_sem=pair_sem.at[1],
        device_id={"fsdp": fs, "tp": sib},
        device_id_type=MESH,
    )
    pair_copy.start()
    pair_copy.wait_recv()
    total = pair_send[...] + pair_recv[...]

    rank = pin.shape[0]
    pairs = rank // 2
    a_in, a_hid = total[:, 0:64], total[:, 64:128]
    rights = (total[:, 128:192], total[:, 192:256], total[:, 256:320])
    row = lax.broadcasted_iota(jnp.int32, (pairs * EX_DEV, rank), 0)
    col = lax.broadcasted_iota(jnp.int32, (pairs * EX_DEV, rank), 1)
    token_row = lax.broadcasted_iota(jnp.int32, (pairs * EX_DEV, tok), 0)
    ids = ids_ref[pl.ds(fs, 1), :]
    mask = (lax.rem(token_row, EX_DEV) == ids).astype(jnp.float32)
    picks = [(col == 2 * (row // EX_DEV) + par).astype(jnp.float32) for par in range(2)]
    left_in = [dot_nt(pick, a_in, highest_precision) * mask for pick in picks]
    left_hid = [dot_nt(pick, a_hid, highest_precision) * mask for pick in picks]
    blank = jnp.zeros((tok, rank), jnp.float32)
    for m in range(3):
        lefts = left_hid if m == 2 else left_in
        g = jnp.dot(
            lefts[0],
            jnp.concatenate([rights[m], blank], axis=1),
            preferred_element_type=jnp.float32,
            precision=highest_precision,
        ) + jnp.dot(
            lefts[1],
            jnp.concatenate([blank, rights[m]], axis=1),
            preferred_element_type=jnp.float32,
            precision=highest_precision,
        )
        gref[pl.ds(m * pairs * EX_DEV, pairs * EX_DEV), :] = g

    block_rows = gsend.shape[1]
    for target in range(n_fsdp):
        chosen = jnp.zeros((block_rows, 128), jnp.float32)
        for b in range(n_fsdp):
            keep = (owner_ref[b] == target).astype(jnp.float32)
            chosen += keep * gref[pl.ds(b * block_rows, block_rows), :]
        gsend[target] = chosen.astype(jnp.bfloat16)
    g_copies = []
    for d in range(1, n_fsdp):
        target = lax.rem(fs + d, n_fsdp)
        copy = pltpu.make_async_remote_copy(
            src_ref=gsend.at[target],
            dst_ref=grecv.at[fs],
            send_sem=g_send_sem.at[d],
            recv_sem=g_recv_sem.at[fs],
            device_id={"fsdp": target, "tp": core},
            device_id_type=MESH,
        )
        copy.start()
        g_copies.append(copy)
    grecv[fs] = gsend[fs]
    small[5].wait()
    for copy in f_copies:
        copy.wait_send()
    pair_copy.wait_send()
    for d in range(1, n_fsdp):
        source = lax.rem(fs + d, n_fsdp)
        place = grecv.at[source]
        pltpu.make_async_copy(place, place, g_recv_sem.at[source]).wait()
    gwide[...] = grecv[...].astype(jnp.float32)
    left = jnp.concatenate(
        [
            jnp.concatenate(
                [gwide[f, p * EX_DEV : (p + 1) * EX_DEV, :] for f in range(n_fsdp)], axis=0
            )
            for p in range(block_rows // EX_DEV)
        ],
        axis=1,
    ).astype(jnp.bfloat16)
    piece = q_vmem.shape[0] // QPIECES
    scores = [
        dot_nt(left, q_vmem[n * piece : (n + 1) * piece, :]) for n in range(QPIECES)
    ]
    for f in range(n_fsdp):
        ssend[f] = jnp.concatenate(
            [score[f * EX_DEV : (f + 1) * EX_DEV, :] for score in scores], axis=0
        ).astype(jnp.bfloat16)

    s_copies = []
    for d in range(1, n_fsdp):
        target = lax.rem(fs + d, n_fsdp)
        copy = pltpu.make_async_remote_copy(
            src_ref=ssend.at[target],
            dst_ref=srecv.at[fs],
            send_sem=s_send_sem.at[d],
            recv_sem=s_recv_sem.at[fs],
            device_id={"fsdp": target, "tp": core},
            device_id_type=MESH,
        )
        copy.start()
        s_copies.append(copy)
    srecv[fs] = ssend[fs]
    for copy in g_copies:
        copy.wait_send()
    for d in range(1, n_fsdp):
        source = lax.rem(fs + d, n_fsdp)
        place = srecv.at[source]
        pltpu.make_async_copy(place, place, s_recv_sem.at[source]).wait()
    summed = jnp.sum(srecv[...].astype(jnp.float32), axis=0)
    for n in range(QPIECES):
        out_ref[:, n * piece : (n + 1) * piece] = summed[n * EX_DEV : (n + 1) * EX_DEV, :]
    for copy in s_copies:
        copy.wait_send()


def fused_shards(n_fsdp, *args):
    x, _, wg = args[:3]
    flat = [a[0].T for a in args[5:7]] + [a.T for a in args[7:10]]
    pin = flat[0]
    q = args[10]
    tok, half = x.shape
    tokens = n_fsdp * tok
    wide = half // SUB
    depth, ff = wg.shape
    rank = pin.shape[0]
    queries, block = q.shape[1:]
    chunks = 2 * SUB
    block_rows = block // 128 * EX_DEV
    dma = pltpu.SemaphoreType.DMA
    bf16, f32 = jnp.bfloat16, jnp.float32
    hbm = pl.BlockSpec(memory_space=pl.ANY)
    return pl.pallas_call(
        functools.partial(fused_kernel, n_fsdp),
        out_shape=jax.ShapeDtypeStruct((EX_DEV, queries), f32),
        in_specs=[hbm] * 11
        + [pl.BlockSpec(memory_space=pltpu.SMEM), pl.BlockSpec(memory_space=pltpu.VMEM)],
        out_specs=pl.BlockSpec(memory_space=pltpu.VMEM),
        scratch_shapes=[
            pltpu.VMEM((chunks, 2, tokens, wide), bf16),
            pltpu.VMEM((3, depth, ff), bf16),
            pltpu.VMEM((queries, block), bf16),
            pltpu.VMEM(pin.shape, bf16),
            pltpu.VMEM(pin.shape, bf16),
            pltpu.VMEM((rank, ff), bf16),
            pltpu.VMEM((rank, ff), bf16),
            pltpu.VMEM((rank, ff), bf16),
            pltpu.VMEM((3, tokens, ff), f32),
            pltpu.VMEM((tokens, 2 * rank), f32),
            pltpu.VMEM((n_fsdp, tok, 2 * rank), f32),
            pltpu.VMEM((tokens, 4 * rank), f32),
            pltpu.VMEM((n_fsdp, tok, 4 * rank), f32),
            pltpu.VMEM((tok, 6 * rank), f32),
            pltpu.VMEM((tok, 6 * rank), f32),
            pltpu.VMEM((n_fsdp * block_rows, 128), f32),
            pltpu.VMEM((n_fsdp, block_rows, 128), bf16),
            pltpu.VMEM((n_fsdp, block_rows, 128), bf16),
            pltpu.VMEM((n_fsdp, block_rows, 128), f32),
            pltpu.VMEM((n_fsdp, QPIECES * EX_DEV, queries // QPIECES), bf16),
            pltpu.VMEM((n_fsdp, QPIECES * EX_DEV, queries // QPIECES), bf16),
            dma((chunks,)),
            dma((3, 2 * SUB)),
            dma((6,)),
            dma((chunks, 4, n_fsdp)),
            dma((chunks, n_fsdp)),
            dma((chunks, n_fsdp)),
            dma((2, n_fsdp)),
            dma((2, n_fsdp)),
            dma((2,)),
            dma((n_fsdp,)),
            dma((n_fsdp,)),
            dma((n_fsdp,)),
            dma((n_fsdp,)),
        ],
        compiler_params=pltpu.CompilerParams(
            collective_id=0, has_side_effects=True, vmem_limit_bytes=62 * 1024 * 1024
        ),
    )(*args[:5], *flat, *args[10:])


def pick_shards(n_fsdp, n_tp):
    def run(*args):
        x, wg, q = args[0], args[2], args[10]
        fits = (
            n_tp == 2
            and n_fsdp == 8
            and x.shape[0] == 16
            and args[7].shape[1] == 64
            and wg.shape[1] % 128 == 0
            and wg.size * 6 + q.size * 2 < 52 * 1024 * 1024
        )
        return fused_shards(n_fsdp, *args) if fits else shards(*args)

    return run


def solution(mesh):
    return jax.shard_map(
        pick_shards(mesh.shape["fsdp"], mesh.shape["tp"]),
        mesh=mesh,
        in_specs=(
            P(("parts", "fsdp"), "tp"),
            P(("parts", "fsdp"), "tp"),
            P(None, ("fsdp", "tp")),
            P(None, ("fsdp", "tp")),
            P(None, ("fsdp", "tp")),
            P("tp", "fsdp", None),
            P("tp", "fsdp", None),
            P(("fsdp", "tp"), None),
            P(("fsdp", "tp"), None),
            P(("fsdp", "tp"), None),
            P("fsdp", "tp", None),
            P(),
            P("parts", None),
        ),
        out_specs=P(("parts", "fsdp"), "tp"),
        check_vma=False,
    )
```

```python
import functools

import jax
import jax.numpy as jnp
from jax import lax
from jax.experimental import pallas as pl
from jax.experimental.pallas import tpu as pltpu
from jax.sharding import PartitionSpec as P

EX_DEV = 4


highest_precision = lax.Precision.HIGHEST


def silu_terms(gate_pre):
    sigmoid_gate = jax.nn.sigmoid(gate_pre)
    return (gate_pre * sigmoid_gate, sigmoid_gate * (1.0 + gate_pre * (1.0 - sigmoid_gate)))


def example_grads(factors, ids, ex_count):
    rank_dim = factors.shape[-1] // 5
    a_in = factors[..., :rank_dim]
    g_out = factors[..., rank_dim : 2 * rank_dim]
    g_gate = factors[..., 2 * rank_dim : 3 * rank_dim]
    g_up = factors[..., 3 * rank_dim : 4 * rank_dim]
    a_hid = factors[..., 4 * rank_dim :]
    one_hot = (ids[:, :, None] == jnp.arange(ex_count, dtype=jnp.int32)[None, None, :]).astype(
        jnp.float32
    )

    def outer_sums(left_side, right_side):
        return jnp.einsum(
            "nte,nti,ntj->neij", one_hot, left_side, right_side, precision=highest_precision
        )

    stacked = jnp.stack(
        [outer_sums(a_in, g_gate), outer_sums(a_in, g_up), outer_sums(a_hid, g_out)], axis=2
    )
    return stacked.reshape(stacked.shape[0] * ex_count, 3 * rank_dim * rank_dim).astype(
        jnp.bfloat16
    )


def matmul(left_side, right_side):
    return jnp.dot(left_side, right_side, preferred_element_type=jnp.float32)


def layer_terms(gate_pre, up_pre, d_hidden, edge_factors, proj_gate, proj_up, proj_hidden):
    silu_gate, silu_slope = silu_terms(gate_pre)
    hidden = (silu_gate * up_pre).astype(jnp.bfloat16)
    d_gate = (d_hidden * up_pre * silu_slope).astype(jnp.bfloat16)
    d_up = (d_hidden * silu_gate).astype(jnp.bfloat16)
    return jnp.concatenate(
        [
            edge_factors,
            matmul(d_gate, proj_gate),
            matmul(d_up, proj_up),
            matmul(hidden, proj_hidden),
        ],
        axis=1,
    )


def shards(
    inputs_x,
    out_grad,
    w_gate,
    w_up,
    w_down,
    proj_input,
    proj_outgrad,
    proj_gate,
    proj_up,
    proj_hidden,
    index_queries,
    block_owner,
    example_ids,
):
    fsdp_pos = lax.axis_index("fsdp")
    core_pos = lax.axis_index("tp")
    half_width = inputs_x.shape[1]
    slice_width = proj_input.shape[1]
    stacked_rows = jnp.stack([inputs_x, out_grad], axis=1)
    p_in = proj_input[0]
    p_out = proj_outgrad[0]
    full_rows = lax.all_gather(stacked_rows, "tp", axis=2, tiled=True)
    edge_start = core_pos * half_width + fsdp_pos * slice_width
    rows_piece = lax.all_gather(full_rows, "fsdp", axis=0, tiled=True)
    x_rows = rows_piece[:, 0]
    dy_rows = rows_piece[:, 1]
    gate_pre = matmul(x_rows, w_gate)
    up_pre = matmul(x_rows, w_up)
    d_hidden = matmul(dy_rows, w_down)
    x_edge = lax.dynamic_slice_in_dim(x_rows, edge_start, slice_width, 1)
    dy_edge = lax.dynamic_slice_in_dim(dy_rows, edge_start, slice_width, 1)
    edge_factors = jnp.concatenate([matmul(x_edge, p_in), matmul(dy_edge, p_out)], axis=1)
    terms_all = layer_terms(
        gate_pre, up_pre, d_hidden, edge_factors, proj_gate, proj_up, proj_hidden
    )
    count_blocks = block_owner.shape[0]
    positions = jnp.arange(count_blocks, dtype=jnp.int32)
    own_factors = lax.psum_scatter(terms_all, ("fsdp", "tp"), scatter_dimension=0, tiled=True)
    device_factors = lax.all_gather(own_factors, "tp", axis=0, tiled=True)
    row_ids = lax.dynamic_slice_in_dim(example_ids, fsdp_pos, 1, 0)
    local_grads = example_grads(device_factors[None], row_ids, EX_DEV)
    inverse = jnp.sum(
        jnp.where(block_owner[:, None] == positions[None, :], positions[:, None], 0), axis=0
    )
    sending = jnp.take(local_grads.reshape(EX_DEV, count_blocks, -1), inverse, axis=1)
    arrived = lax.all_to_all(sending, "fsdp", split_axis=1, concat_axis=0, tiled=True)
    received = arrived.reshape(arrived.shape[0], arrived.shape[2])
    query_block = index_queries[0]
    return lax.psum_scatter(
        lax.dot_general(
            received, query_block, (((1,), (1,)), ((), ())), preferred_element_type=jnp.float32
        ),
        "fsdp",
        scatter_dimension=0,
        tiled=True,
    )


MESH = pl.DeviceIdType.MESH
NY = 2
SUB = 2
QPIECES = 4
SKEW = 1
LAG = 1
PER = 1


def dot_nt(left_side, right_side, precision=None):
    return lax.dot_general(
        left_side,
        right_side,
        (((1,), (1,)), ((), ())),
        preferred_element_type=jnp.float32,
        precision=precision,
    )


def fused_kernel(
    n_fsdp,
    x_hbm,
    dy_hbm,
    wg_hbm,
    wu_hbm,
    wd_hbm,
    pin_hbm,
    pout_hbm,
    pg_hbm,
    pu_hbm,
    ph_hbm,
    q_hbm,
    owner_ref,
    ids_ref,
    out_ref,
    rows,
    w_vmem,
    q_vmem,
    pin,
    pout,
    pg,
    pu,
    ph,
    acc,
    early_send,
    early_recv,
    late_send,
    late_recv,
    pair_send,
    pair_recv,
    gref,
    gsend,
    grecv,
    gwide,
    ssend,
    srecv,
    own_sem,
    w_sem,
    small_sem,
    gather_send,
    gather_recv,
    sib_recv,
    f_send_sem,
    f_recv_sem,
    pair_sem,
    g_send_sem,
    g_recv_sem,
    s_send_sem,
    s_recv_sem,
):
    fs = lax.axis_index("fsdp")
    core = lax.axis_index("tp")
    sib = 1 - core
    nz = n_fsdp // NY
    z = fs // NY
    y = lax.rem(fs, NY)
    tok = x_hbm.shape[0]
    wide = rows.shape[-1]
    chunks = 2 * SUB
    ff = wg_hbm.shape[1]

    own_copies = []
    for c in range(chunks):
        source = x_hbm if c < SUB else dy_hbm
        s = c % SUB
        copy = pltpu.make_async_copy(
            source.at[:, pl.ds(s * wide, wide)],
            rows.at[c, core, pl.ds(fs * tok, tok), :],
            own_sem.at[c],
        )
        copy.start()
        own_copies.append(copy)

    def weight_copy(matrix, hbm, s, h):
        span = pl.ds((h * SUB + s) * wide, wide)
        return pltpu.make_async_copy(
            hbm.at[span, :], w_vmem.at[matrix, span, :], w_sem.at[matrix, s * 2 + h]
        )

    weights = {}
    for s in range(SUB):
        for h in range(2):
            for matrix, hbm in ((0, wg_hbm), (1, wu_hbm)):
                weights[matrix, s, h] = weight_copy(matrix, hbm, s, h)
                weights[matrix, s, h].start()
    small = [
        pltpu.make_async_copy(a, b, small_sem.at[i])
        for i, (a, b) in enumerate(
            (
                (pin_hbm, pin),
                (pout_hbm, pout),
                (pg_hbm, pg),
                (pu_hbm, pu),
                (ph_hbm, ph),
                (q_hbm.at[0], q_vmem),
            )
        )
    ]
    for copy in small[:5]:
        copy.start()
    for s in range(SUB):
        for h in range(2):
            weights[2, s, h] = weight_copy(2, wd_hbm, s, h)
            weights[2, s, h].start()
    small[5].start()

    barrier = pltpu.get_barrier_semaphore()
    peers = [(d, t) for d in range(n_fsdp) for t in range(2) if d or t]
    for d, t in peers:
        pl.semaphore_signal(
            barrier,
            inc=1,
            device_id={"fsdp": lax.rem(fs + d, n_fsdp), "tp": lax.rem(core + t, 2)},
            device_id_type=MESH,
        )
    pl.semaphore_wait(barrier, len(peers))

    UP, DOWN, ACROSS, SIB = 0, 1, 2, 3

    def piece_copy(c, origin, way):
        target_fs = {UP: fs + NY, DOWN: fs - NY, ACROSS: z * NY + (1 - y), SIB: fs}[way]
        place = rows.at[c, core, pl.ds(origin * tok, tok), :]
        return pltpu.make_async_remote_copy(
            src_ref=place,
            dst_ref=place,
            send_sem=gather_send.at[c, way, origin],
            recv_sem=(sib_recv if way == SIB else gather_recv).at[c, origin],
            device_id={"fsdp": target_fs, "tp": sib if way == SIB else core},
            device_id_type=MESH,
        )

    def wait_piece(c, origin):
        place = rows.at[c, core, pl.ds(origin * tok, tok), :]
        pltpu.make_async_copy(place, place, gather_recv.at[c, origin]).wait()

    def goes_across(c, at, origin_z):
        if c % 2 == 0:
            return at >= 0
        low = (origin_z == 0) & ((at == 1) | (at == nz - 1))
        high = (origin_z == nz - 1) & ((at == nz - 2) | (at == 0))
        return jnp.logical_not(low | high)

    def send_own(c):
        own_copies[c].wait()
        piece_copy(c, fs, ACROSS).start()

        @pl.when(z < nz - 1)
        def _():
            piece_copy(c, fs, UP).start()

        @pl.when(z > 0)
        def _():
            piece_copy(c, fs, DOWN).start()

        piece_copy(c, fs, SIB).start()

    def forward_step(c, d):
        if d < nz:

            @pl.when(z - d >= 0)
            def _():
                origin = fs - d * NY
                wait_piece(c, origin)

                @pl.when(z < nz - 1)
                def _():
                    piece_copy(c, origin, UP).start()

                @pl.when(goes_across(c, z, z - d))
                def _():
                    piece_copy(c, origin, ACROSS).start()

                piece_copy(c, origin, SIB).start()

            @pl.when(z + d < nz)
            def _():
                origin = fs + d * NY
                wait_piece(c, origin)

                @pl.when(z > 0)
                def _():
                    piece_copy(c, origin, DOWN).start()

                @pl.when(goes_across(c, z, z + d))
                def _():
                    piece_copy(c, origin, ACROSS).start()

                piece_copy(c, origin, SIB).start()

        beside = z * NY + (1 - y)
        back = d - 1

        @pl.when(z - back >= 0)
        def _():
            origin = beside - back * NY
            wait_piece(c, origin)
            if c % 2 and back in (0, nz - 2):

                @pl.when(z == back)
                def _():
                    piece_copy(c, origin, UP).start()

            if c % 2 and back == 0:

                @pl.when(z == nz - 1)
                def _():
                    piece_copy(c, origin, DOWN).start()

            piece_copy(c, origin, SIB).start()

        if back:

            @pl.when(z + back < nz)
            def _():
                origin = beside + back * NY
                wait_piece(c, origin)
                if c % 2 and back == nz - 2:

                    @pl.when(z == 1)
                    def _():
                        piece_copy(c, origin, DOWN).start()

                piece_copy(c, origin, SIB).start()

    def wait_sib(c):
        for origin in range(n_fsdp):
            place = rows.at[c, sib, pl.ds(origin * tok, tok), :]
            pltpu.make_async_copy(place, place, sib_recv.at[c, origin]).wait()

    def drain_sends(c):
        for origin in range(n_fsdp):
            oz, oy = origin // NY, origin % NY
            piece_copy(c, origin, SIB).wait_send()

            @pl.when(y == oy)
            def _():

                @pl.when(goes_across(c, z, oz))
                def _():
                    piece_copy(c, origin, ACROSS).wait_send()

                @pl.when((z >= oz) & (z < nz - 1))
                def _():
                    piece_copy(c, origin, UP).wait_send()

                @pl.when((z <= oz) & (z > 0))
                def _():
                    piece_copy(c, origin, DOWN).wait_send()

            if c % 2 and oz == 0:

                @pl.when((y != oy) & ((z == 0) | (z == nz - 2)))
                def _():
                    piece_copy(c, origin, UP).wait_send()

            if c % 2 and oz == nz - 1:

                @pl.when((y != oy) & ((z == nz - 1) | (z == 1)))
                def _():
                    piece_copy(c, origin, DOWN).wait_send()

    parts = nz
    tile = 512
    tiles = wide // tile

    def multiply(c, part):
        s = c % SUB
        per = 2 // SUB if SUB > 2 else 1
        h, rest = divmod(part, parts // 2)
        share = tiles // (parts // 2)
        matrices = (0, 1) if c < SUB else (2,)
        if rest == 0:
            for matrix in matrices:
                weights[matrix, s, h].wait()

        def body(k, carry):
            start = pl.multiple_of((rest * share + k) * tile, tile)
            left = rows[c, h, :, pl.ds(start, tile)]
            for matrix in matrices:
                base = pl.multiple_of((h * SUB + s) * wide + start, tile)
                acc[matrix] += matmul(left, w_vmem[matrix, pl.ds(base, tile), :])
            return carry

        lax.fori_loop(0, share, body, 0)

    def edge(first_chunk):
        width = pin.shape[1]
        per = wide // width
        at = pl.multiple_of(lax.rem(fs, per) * width, width)
        return rows[first_chunk + fs // per, core, :, pl.ds(at, width)]

    f_copies = []

    def send_factors(src, dst, stage):
        for d in range(1, n_fsdp):
            target = lax.rem(fs + d, n_fsdp)
            copy = pltpu.make_async_remote_copy(
                src_ref=src.at[pl.ds(target * tok, tok), :],
                dst_ref=dst.at[fs],
                send_sem=f_send_sem.at[stage, d],
                recv_sem=f_recv_sem.at[stage, fs],
                device_id={"fsdp": target, "tp": core},
                device_id_type=MESH,
            )
            copy.start()
            f_copies.append(copy)
        dst[fs] = src[pl.ds(fs * tok, tok), :]

    def arrive_factors(dst, stage):
        for d in range(1, n_fsdp):
            source = lax.rem(fs + d, n_fsdp)
            place = dst.at[source]
            pltpu.make_async_copy(place, place, f_recv_sem.at[stage, source]).wait()

    cols = 128

    def middle():
        for copy in small[:5]:
            copy.wait()
        a_hid = jnp.zeros((n_fsdp * tok, ph.shape[0]), jnp.float32)
        for n in range(ff // cols):
            at = slice(n * cols, (n + 1) * cols)
            gate = acc[0, :, at]
            up = acc[1, :, at]
            silu_gate, slope = silu_terms(gate)
            a_hid += dot_nt((silu_gate * up).astype(jnp.bfloat16), ph[:, at])
            acc[0, :, at] = up * slope
            acc[1, :, at] = silu_gate
        a_in = dot_nt(edge(0), pin[...])
        early_send[...] = jnp.concatenate([a_in, a_hid], axis=1)
        send_factors(early_send, early_recv, 0)

    def run_unit(c, part):
        if part == 0:
            wait_sib(c)
        multiply(c, part)
        if c == SUB - 1 and part == parts - 1:
            middle()

    acc[...] = jnp.zeros_like(acc)
    for c in range(chunks):
        send_own(c)
    order = sorted(
        (d + SKEW * c, c, d) for c in range(chunks) for d in range(1, nz + 1)
    )
    ready = []
    work = []
    for _, c, d in order:
        ready.append((c, d))
        forward_step(c, d)
        if len(ready) > LAG and ready[-1 - LAG][1] == nz:
            done = ready[-1 - LAG][0]
            work += [(done, part) for part in range(parts)]
        for _ in range(PER):
            if work:
                run_unit(*work.pop(0))
    for c, d in ready[-LAG:]:
        if d == nz:
            work += [(c, part) for part in range(parts)]
    for unit in work:
        run_unit(*unit)
    g_out = dot_nt(edge(SUB), pout[...])
    g_gate = jnp.zeros_like(g_out)
    g_up = jnp.zeros_like(g_out)
    for n in range(ff // cols):
        at = slice(n * cols, (n + 1) * cols)
        d_hidden = acc[2, :, at]
        g_gate += dot_nt((d_hidden * acc[0, :, at]).astype(jnp.bfloat16), pg[:, at])
        g_up += dot_nt((d_hidden * acc[1, :, at]).astype(jnp.bfloat16), pu[:, at])
    late_send[:, 0:128] = jnp.concatenate([g_gate, g_up], axis=1)
    late_send[:, 128:256] = jnp.concatenate([g_out, jnp.zeros_like(g_out)], axis=1)

    send_factors(late_send, late_recv, 1)
    for c in range(chunks):
        drain_sends(c)
    arrive_factors(early_recv, 0)
    pair_send[:, 0:128] = jnp.sum(early_recv[...], axis=0)
    arrive_factors(late_recv, 1)
    pair_send[:, 128:384] = jnp.sum(late_recv[...], axis=0)
    pair_copy = pltpu.make_async_remote_copy(
        src_ref=pair_send,
        dst_ref=pair_recv,
        send_sem=pair_sem.at[0],
        recv_sem=pair_sem.at[1],
        device_id={"fsdp": fs, "tp": sib},
        device_id_type=MESH,
    )
    pair_copy.start()
    pair_copy.wait_recv()
    total = pair_send[...] + pair_recv[...]

    rank = pin.shape[0]
    pairs = rank // 2
    a_in, a_hid = total[:, 0:64], total[:, 64:128]
    rights = (total[:, 128:192], total[:, 192:256], total[:, 256:320])
    row = lax.broadcasted_iota(jnp.int32, (pairs * EX_DEV, rank), 0)
    col = lax.broadcasted_iota(jnp.int32, (pairs * EX_DEV, rank), 1)
    token_row = lax.broadcasted_iota(jnp.int32, (pairs * EX_DEV, tok), 0)
    ids = ids_ref[pl.ds(fs, 1), :]
    mask = (lax.rem(token_row, EX_DEV) == ids).astype(jnp.float32)
    picks = [(col == 2 * (row // EX_DEV) + par).astype(jnp.float32) for par in range(2)]
    left_in = [dot_nt(pick, a_in, highest_precision) * mask for pick in picks]
    left_hid = [dot_nt(pick, a_hid, highest_precision) * mask for pick in picks]
    blank = jnp.zeros((tok, rank), jnp.float32)
    for m in range(3):
        lefts = left_hid if m == 2 else left_in
        g = jnp.dot(
            lefts[0],
            jnp.concatenate([rights[m], blank], axis=1),
            preferred_element_type=jnp.float32,
            precision=highest_precision,
        ) + jnp.dot(
            lefts[1],
            jnp.concatenate([blank, rights[m]], axis=1),
            preferred_element_type=jnp.float32,
            precision=highest_precision,
        )
        gref[pl.ds(m * pairs * EX_DEV, pairs * EX_DEV), :] = g

    block_rows = gsend.shape[1]
    for target in range(n_fsdp):
        chosen = jnp.zeros((block_rows, 128), jnp.float32)
        for b in range(n_fsdp):
            keep = (owner_ref[b] == target).astype(jnp.float32)
            chosen += keep * gref[pl.ds(b * block_rows, block_rows), :]
        gsend[target] = chosen.astype(jnp.bfloat16)
    g_copies = []
    for d in range(1, n_fsdp):
        target = lax.rem(fs + d, n_fsdp)
        copy = pltpu.make_async_remote_copy(
            src_ref=gsend.at[target],
            dst_ref=grecv.at[fs],
            send_sem=g_send_sem.at[d],
            recv_sem=g_recv_sem.at[fs],
            device_id={"fsdp": target, "tp": core},
            device_id_type=MESH,
        )
        copy.start()
        g_copies.append(copy)
    grecv[fs] = gsend[fs]
    small[5].wait()
    for copy in f_copies:
        copy.wait_send()
    pair_copy.wait_send()
    for d in range(1, n_fsdp):
        source = lax.rem(fs + d, n_fsdp)
        place = grecv.at[source]
        pltpu.make_async_copy(place, place, g_recv_sem.at[source]).wait()
    gwide[...] = grecv[...].astype(jnp.float32)
    left = jnp.concatenate(
        [
            jnp.concatenate(
                [gwide[f, p * EX_DEV : (p + 1) * EX_DEV, :] for f in range(n_fsdp)], axis=0
            )
            for p in range(block_rows // EX_DEV)
        ],
        axis=1,
    ).astype(jnp.bfloat16)
    piece = q_vmem.shape[0] // QPIECES
    scores = [
        dot_nt(left, q_vmem[n * piece : (n + 1) * piece, :]) for n in range(QPIECES)
    ]
    for f in range(n_fsdp):
        ssend[f] = jnp.concatenate(
            [score[f * EX_DEV : (f + 1) * EX_DEV, :] for score in scores], axis=0
        ).astype(jnp.bfloat16)

    s_copies = []
    for d in range(1, n_fsdp):
        target = lax.rem(fs + d, n_fsdp)
        copy = pltpu.make_async_remote_copy(
            src_ref=ssend.at[target],
            dst_ref=srecv.at[fs],
            send_sem=s_send_sem.at[d],
            recv_sem=s_recv_sem.at[fs],
            device_id={"fsdp": target, "tp": core},
            device_id_type=MESH,
        )
        copy.start()
        s_copies.append(copy)
    srecv[fs] = ssend[fs]
    for copy in g_copies:
        copy.wait_send()
    for d in range(1, n_fsdp):
        source = lax.rem(fs + d, n_fsdp)
        place = srecv.at[source]
        pltpu.make_async_copy(place, place, s_recv_sem.at[source]).wait()
    summed = jnp.sum(srecv[...].astype(jnp.float32), axis=0)
    for n in range(QPIECES):
        out_ref[:, n * piece : (n + 1) * piece] = summed[n * EX_DEV : (n + 1) * EX_DEV, :]
    for copy in s_copies:
        copy.wait_send()


def fused_shards(n_fsdp, *args):
    x, _, wg = args[:3]
    flat = [a[0].T for a in args[5:7]] + [a.T for a in args[7:10]]
    pin = flat[0]
    q = args[10]
    tok, half = x.shape
    tokens = n_fsdp * tok
    wide = half // SUB
    depth, ff = wg.shape
    rank = pin.shape[0]
    queries, block = q.shape[1:]
    chunks = 2 * SUB
    block_rows = block // 128 * EX_DEV
    dma = pltpu.SemaphoreType.DMA
    bf16, f32 = jnp.bfloat16, jnp.float32
    hbm = pl.BlockSpec(memory_space=pl.ANY)
    return pl.pallas_call(
        functools.partial(fused_kernel, n_fsdp),
        out_shape=jax.ShapeDtypeStruct((EX_DEV, queries), f32),
        in_specs=[hbm] * 11
        + [pl.BlockSpec(memory_space=pltpu.SMEM), pl.BlockSpec(memory_space=pltpu.VMEM)],
        out_specs=pl.BlockSpec(memory_space=pltpu.VMEM),
        scratch_shapes=[
            pltpu.VMEM((chunks, 2, tokens, wide), bf16),
            pltpu.VMEM((3, depth, ff), bf16),
            pltpu.VMEM((queries, block), bf16),
            pltpu.VMEM(pin.shape, bf16),
            pltpu.VMEM(pin.shape, bf16),
            pltpu.VMEM((rank, ff), bf16),
            pltpu.VMEM((rank, ff), bf16),
            pltpu.VMEM((rank, ff), bf16),
            pltpu.VMEM((3, tokens, ff), f32),
            pltpu.VMEM((tokens, 2 * rank), f32),
            pltpu.VMEM((n_fsdp, tok, 2 * rank), f32),
            pltpu.VMEM((tokens, 4 * rank), f32),
            pltpu.VMEM((n_fsdp, tok, 4 * rank), f32),
            pltpu.VMEM((tok, 6 * rank), f32),
            pltpu.VMEM((tok, 6 * rank), f32),
            pltpu.VMEM((n_fsdp * block_rows, 128), f32),
            pltpu.VMEM((n_fsdp, block_rows, 128), bf16),
            pltpu.VMEM((n_fsdp, block_rows, 128), bf16),
            pltpu.VMEM((n_fsdp, block_rows, 128), f32),
            pltpu.VMEM((n_fsdp, QPIECES * EX_DEV, queries // QPIECES), bf16),
            pltpu.VMEM((n_fsdp, QPIECES * EX_DEV, queries // QPIECES), bf16),
            dma((chunks,)),
            dma((3, 2 * SUB)),
            dma((6,)),
            dma((chunks, 4, n_fsdp)),
            dma((chunks, n_fsdp)),
            dma((chunks, n_fsdp)),
            dma((2, n_fsdp)),
            dma((2, n_fsdp)),
            dma((2,)),
            dma((n_fsdp,)),
            dma((n_fsdp,)),
            dma((n_fsdp,)),
            dma((n_fsdp,)),
        ],
        compiler_params=pltpu.CompilerParams(
            collective_id=0, has_side_effects=True, vmem_limit_bytes=62 * 1024 * 1024
        ),
    )(*args[:5], *flat, *args[10:])


def pick_shards(n_fsdp, n_tp):
    def run(*args):
        x, wg, q = args[0], args[2], args[10]
        fits = (
            n_tp == 2
            and n_fsdp == 8
            and x.shape[0] == 16
            and args[7].shape[1] == 64
            and wg.shape[1] % 128 == 0
            and wg.size * 6 + q.size * 2 < 52 * 1024 * 1024
        )
        return fused_shards(n_fsdp, *args) if fits else shards(*args)

    return run


def solution(mesh):
    return jax.shard_map(
        pick_shards(mesh.shape["fsdp"], mesh.shape["tp"]),
        mesh=mesh,
        in_specs=(
            P(("parts", "fsdp"), "tp"),
            P(("parts", "fsdp"), "tp"),
            P(None, ("fsdp", "tp")),
            P(None, ("fsdp", "tp")),
            P(None, ("fsdp", "tp")),
            P("tp", "fsdp", None),
            P("tp", "fsdp", None),
            P(("fsdp", "tp"), None),
            P(("fsdp", "tp"), None),
            P(("fsdp", "tp"), None),
            P("fsdp", "tp", None),
            P(),
            P("parts", None),
        ),
        out_specs=P(("parts", "fsdp"), "tp"),
        check_vma=False,
    )
```
